32 devices in a mesh: groups: 2 (over y), replica: 16 (over z, x, core).
Axes of the slice: x: 2, y: 2, z: 4, core: 2. Of those that a mesh axis runs over, the one named last changes fastest.
Arguments:
- hidden_state_rows: bfloat16 [3072, 8192], P(('groups', 'replica')), parts along dimension 0, may hold values from -6 to 6
- base_queries: bfloat16 [3072, 4096], P(('groups', 'replica')), parts along dimension 0, may hold values from -6 to 6
- cached_key_rows: bfloat16 [3072, 32, 512], P(('groups', 'replica')), parts along dimension 0, may hold values from -600 to 600
- cached_value_rows: bfloat16 [3072, 32, 512], P(('groups', 'replica')), parts along dimension 0, may hold values from -6 to 6
- cache_lengths: int32 [3072], P(('groups', 'replica')), parts along dimension 0, may hold values from 16 to 32, as said below
- joining_flags: int32 [3072], P(('groups', 'replica')), parts along dimension 0, may hold values 0 or 1
- adapter_index: int32 [3072, 1], P(('groups', 'replica')), parts along dimension 0, may hold values from 0 to 15; in each aligned block of 96 rows (0 to 95, 96 to 191, ...) at most 12 rows name the same one
- adapter_owner_row: int32 [16], replicated, may hold values from 0 to 15, each once
- pair_trade_flags: int32 [16], P('groups'), parts along dimension 0, may hold values 0 or 1
- down_factors: bfloat16 [16, 8192, 64], P('replica'), may hold values from -0.0625 to 0.0625
- up_factors: bfloat16 [16, 64, 4096], P('replica'), may hold values from -0.75 to 0.75
Outputs:
- attn_out: bfloat16 [3072, 4096], P(('groups', 'replica')), parts along dimension 0
The draws below stay inside these ranges and needn't reach their ends.
There are 2 independent parts, one for each index of `groups`. The reference program is written for one: setup_inputs(seed, part) draws one part's arguments, and reference() takes and returns one part's arrays. A program takes and returns all parts, laid end to end along the dimension named above; an argument that names none is the same for every part. Nothing has to cross between parts.
Inputs may be any that keep to these rules, and one draw needn't show every extreme that they name: `adapter_index`: within the requests of one replica (aligned blocks of 96 rows) no adapter is named more than 12 times, a bound that some block reaches. `adapter_owner_row`: A permutation of the adapters. `cache_lengths`: the first request of each replica has 32 live positions, the second 16.
All inputs are finite; a program needn't handle non-finite values. No bound on the sum of `joining_flags` on one device may be relied on, other than what follows from the above.
Results may differ from the reference program's by a relative error of at most 0.0052.
Values may be sent and summed in bfloat16 or wider, within the bound.
A program may use at most 64 MiB of HBM per device.

```python
import math
import jax
import jax.numpy as jnp
import numpy as np
from jax import lax

MODEL_WIDTH = 8192
QUERY_HEADS = 32
KEY_HEADS = 4
HEAD_WIDTH = 128
ADAPTER_RANK = 64
REQ_DEV = 96
CONTEXT_SLOTS = 32
SPAN = 16
CAP = 12
ADAPTER_COUNT = 16
REQUEST_COUNT = 1536
N_REPLICA = 16


def shared_draws(key):
    key_query, key_length = jax.random.split(key, 2)
    query_rows = jnp.clip(jax.random.normal(key_query, (REQUEST_COUNT, QUERY_HEADS * HEAD_WIDTH), jnp.float32), -6.0, 6.0)
    lengths = jax.random.randint(key_length, (N_REPLICA, REQ_DEV), SPAN, CONTEXT_SLOTS + 1)
    lengths = lengths.at[:, 0].set(CONTEXT_SLOTS).at[:, 1].set(SPAN)
    return (query_rows, lengths.reshape(REQUEST_COUNT).astype(jnp.int32))


def draw_base_queries(key, part):
    query_rows, lengths = shared_draws(key)
    return query_rows.astype(jnp.bfloat16)


def draw_cache_lengths(key, part):
    query_rows, lengths = shared_draws(key)
    return lengths


def draw_cached_key_rows(key, part):
    key = jax.random.fold_in(key, 7)
    flat_keys = jax.random.fold_in(key, 0)
    flat_values = jnp.clip(jax.random.normal(flat_keys, (REQUEST_COUNT, CONTEXT_SLOTS, KEY_HEADS * HEAD_WIDTH), jnp.float32), -6.0, 6.0)
    return flat_values.astype(jnp.bfloat16)


def touch_ends(values, stream_key, low, high):
    longest = values.shape.index(max(values.shape))
    spots = []
    for shift in (0, 1):
        where = [jax.random.randint(jax.random.fold_in(stream_key, axis), (), 0, length) for axis, length in enumerate(values.shape)]
        where[longest] = (where[longest] + shift) % values.shape[longest]
        spots.append(tuple(where))
    return values.at[spots[0]].set(low).at[spots[1]].set(high)


def steps_of(stream_key, extent, pieces, least, top_value):
    level = 1.0
    for axis_at, parts in pieces:
        heights = jax.random.uniform(jax.random.fold_in(jax.random.fold_in(stream_key, 6), axis_at), (parts,), jnp.float32, least / len(pieces), top_value / len(pieces))
        level = level * jnp.repeat(jnp.exp(heights), extent[axis_at] // parts).reshape((-1,) + (1,) * (len(extent) - 1 - axis_at))
    return level


def shared_out(rng, own, number, rows, count, top, limit, slope):
    sequence = jax.random.permutation(rng, count)
    crowded, common = portions_of(count, rows * top, limit, slope, True), portions_of(count, rows * top, limit, slope, False)
    places = jnp.arange(count)

    def named(sizes, turn):
        used = int((sizes > 0).sum())
        fixed = max(1, used // 4)
        moved = fixed + (places - fixed + turn * (used - fixed)) % max(1, count - fixed)
        return jnp.zeros((count,), jnp.int32).at[sequence[jnp.where(places < fixed, places, moved)]].set(jnp.asarray(sizes, jnp.int32))

    sizes = jnp.where(number % 4 == 0, named(crowded, number // 4), named(common, number - number // 4 - 1))
    mixed = jax.random.permutation(jax.random.fold_in(own, 3), count)
    giver, sink = mixed[0:count // 2 * 2:2], mixed[1:count // 2 * 2:2]
    room = jnp.minimum(sizes[giver] - 1, limit - sizes[sink]) // 2
    room = jnp.where((giver == sequence[0]) | (sink == sequence[0]) | (sizes[sink] == 0), 0, jnp.maximum(room, 0))
    moved = jax.random.randint(jax.random.fold_in(own, 4), (count // 2,), 0, 1 << 20) % (room + 1)
    sizes = sizes.at[giver].add(-moved).at[sink].add(moved)
    items = jnp.searchsorted(jnp.cumsum(sizes), jnp.arange(rows * top), side="right").astype(jnp.int32)
    grid = items.reshape(top, rows).T
    grid = grid[jax.random.permutation(jax.random.fold_in(own, 1), rows)]
    turn = jax.random.randint(jax.random.fold_in(own, 2), (rows, 1), 0, top)
    return jnp.take_along_axis(grid, (jnp.arange(top)[None, :] + turn) % top, axis=1)


def portions_of(number_of, total, most, slope, full):
    portions = [(1 << 20) // math.isqrt(standing ** slope) + 1 for standing in range(1, number_of + 1)]
    largest = most if full else min(most, max(-(-total // number_of), total * portions[0] // sum(portions)))
    least = 1 if total - largest >= number_of - 1 else 0
    counts, rest = [largest] + [least] * (number_of - 1), total - largest - least * (number_of - 1)
    while rest > 0:
        movable = [i for i in range(1, number_of) if counts[i] < largest] or [i for i in range(1, number_of) if counts[i] < most]
        pool, remaining = sum([portions[i] for i in movable]), rest
        for i in movable:
            extra = min(most - counts[i], max(1, remaining * portions[i] // pool), rest)
            counts[i] = counts[i] + extra
            rest = rest - extra
    return np.array(counts)


def bell_draw(stream_key, shape, spread, most, shards=(), kind=jnp.bfloat16):
    drawn = spread * jax.random.normal(stream_key, shape, jnp.float32)
    if shards:
        drawn = drawn * steps_of(stream_key, shape, shards, -0.22, 0.18)
    return jnp.clip(drawn, -most, most).astype(kind)


def setup_inputs(seed: int = 0, part: int = 0) -> dict:
    seeds = jax.random.split(jax.random.key(seed), 12)
    part_keys = jax.random.split(jax.random.fold_in(seeds[11], part), 12)
    hidden_state_rows = bell_draw(part_keys[0], (REQUEST_COUNT, MODEL_WIDTH), 1.0, 6.0, ((0, 16),))
    base_queries = draw_base_queries(jax.random.fold_in(jax.random.fold_in(seeds[11], part), 71), part)
    cached_key_rows = draw_cached_key_rows(jax.random.fold_in(jax.random.fold_in(seeds[11], part), 71), part)
    cached_value_rows = bell_draw(part_keys[3], (REQUEST_COUNT, CONTEXT_SLOTS, KEY_HEADS * HEAD_WIDTH), 1.0, 6.0, ((0, 16),))
    cache_lengths = draw_cache_lengths(jax.random.fold_in(jax.random.fold_in(seeds[11], part), 71), part)
    joining_flags = touch_ends((jax.random.randint(part_keys[5], (REQUEST_COUNT,), 0, 3) < 1).astype(jnp.int32), jax.random.fold_in(part_keys[5], 1), 0, 1)
    adapter_index_keys = jax.random.split(jax.random.fold_in(part_keys[6], 1), REQUEST_COUNT // REQ_DEV)
    adapter_index_turns = jax.random.permutation(jax.random.fold_in(part_keys[6], 3), REQUEST_COUNT // REQ_DEV)
    adapter_index = jax.vmap(lambda own, number: shared_out(jax.random.fold_in(part_keys[6], 2), own, number, REQ_DEV, ADAPTER_COUNT, 1, CAP, 2))(adapter_index_keys, adapter_index_turns).reshape((REQUEST_COUNT, 1))
    adapter_owner_row = jax.random.permutation(seeds[7], ADAPTER_COUNT).astype(jnp.int32)
    pair_trade_flags = touch_ends((jax.random.randint(part_keys[8], (N_REPLICA // 2,), 0, 2) < 1).astype(jnp.int32), jax.random.fold_in(part_keys[8], 1), 0, 1)
    down_factors = bell_draw(seeds[9], (ADAPTER_COUNT, MODEL_WIDTH, ADAPTER_RANK), MODEL_WIDTH ** -0.5, 0.0625, ((0, 16),))
    up_factors = bell_draw(seeds[10], (ADAPTER_COUNT, ADAPTER_RANK, QUERY_HEADS * HEAD_WIDTH), ADAPTER_RANK ** -0.5, 0.75, ((0, 16),))
    return {"hidden_state_rows": hidden_state_rows, "base_queries": base_queries, "cached_key_rows": cached_key_rows, "cached_value_rows": cached_value_rows, "cache_lengths": cache_lengths, "joining_flags": joining_flags, "adapter_index": adapter_index, "adapter_owner_row": adapter_owner_row, "pair_trade_flags": pair_trade_flags, "down_factors": down_factors, "up_factors": up_factors}


ADAPTER_SCALE = 0.5
NEG_LARGE = -1e+30

def attend(base_queries, query_shift, cached_key_rows, cached_value_rows, cache_lengths, joining_flags):
    total_rows = base_queries.shape[0]
    cache_positions = cached_key_rows.shape[1]
    heads_per_group = QUERY_HEADS // KEY_HEADS
    base_share = base_queries.reshape(total_rows, KEY_HEADS, heads_per_group, HEAD_WIDTH).astype(jnp.float32)
    adapter_share = query_shift.reshape(total_rows, KEY_HEADS, heads_per_group, HEAD_WIDTH).astype(jnp.float32)
    keys_from_cache = cached_key_rows.reshape(total_rows, cache_positions, KEY_HEADS, HEAD_WIDTH).astype(jnp.float32)
    values_from_cache = cached_value_rows.reshape(total_rows, cache_positions, KEY_HEADS, HEAD_WIDTH).astype(jnp.float32)
    scores = jnp.einsum('rkgd,rpkd->rkgp', base_share, keys_from_cache)
    scores = scores + jnp.einsum('rkgd,rpkd->rkgp', adapter_share, keys_from_cache)
    scores = scores / math.sqrt(HEAD_WIDTH)
    position = jnp.arange(cache_positions, dtype=jnp.int32)[None, :]
    limits = cache_lengths[:, None]
    visible = (position < limits) & ((joining_flags[:, None] == 0) | (position >= limits - SPAN))
    visible = visible[:, None, None, :]
    masked = jnp.where(visible, scores, NEG_LARGE)
    row_top = lax.optimization_barrier(jnp.max(masked, axis=-1, keepdims=True))
    raised = jnp.where(visible, jnp.exp(masked - row_top), 0.0)
    weights = (raised / lax.optimization_barrier(jnp.sum(raised, axis=-1, keepdims=True))).astype(jnp.bfloat16)
    mixed_out = jnp.einsum('rkgp,rpkd->rkgd', weights.astype(jnp.float32), values_from_cache)
    return mixed_out.astype(jnp.bfloat16).reshape(total_rows, QUERY_HEADS * HEAD_WIDTH)

def adapter_shift(hidden_state_rows, adapter_index, adapter_owner_row, down_factors, up_factors):
    stores = adapter_owner_row[adapter_index[:, 0]].astype(jnp.int32)

    def per_row(packed):
        single_row, adapter_store = packed
        narrowed_rows = jnp.dot(single_row[None, :], down_factors[adapter_store], preferred_element_type=jnp.float32).astype(jnp.bfloat16)
        widened_rows = ADAPTER_SCALE * jnp.dot(narrowed_rows, up_factors[adapter_store], preferred_element_type=jnp.float32)
        return widened_rows[0].astype(jnp.bfloat16)
    return lax.map(per_row, (hidden_state_rows, stores))

def as_blocks(array):
    return array.reshape((N_REPLICA, REQ_DEV) + array.shape[1:])

def reference(hidden_state_rows, base_queries, cached_key_rows, cached_value_rows, cache_lengths, joining_flags, adapter_index, adapter_owner_row, pair_trade_flags, down_factors, up_factors):
    query_shift = adapter_shift(hidden_state_rows, adapter_index, adapter_owner_row, down_factors, up_factors)

    def per_block(packed):
        return attend(packed[0], packed[1], packed[2], packed[3], packed[4], packed[5])
    blocks = lax.map(per_block, (as_blocks(base_queries), as_blocks(query_shift), as_blocks(cached_key_rows), as_blocks(cached_value_rows), as_blocks(cache_lengths), as_blocks(joining_flags)))
    paired = blocks.reshape(N_REPLICA // 2, 2, REQ_DEV, QUERY_HEADS * HEAD_WIDTH)
    flipped = paired[:, ::-1]
    placed = jnp.where(pair_trade_flags[:, None, None, None] == 1, flipped, paired)
    return placed.reshape(N_REPLICA * REQ_DEV, QUERY_HEADS * HEAD_WIDTH)
```

```python
import functools
import math

import jax
import jax.numpy as jnp
from jax import lax
from jax.experimental import pallas as pl
from jax.experimental.pallas import tpu as pltpu
from jax.sharding import PartitionSpec as P

QUERY_HEADS = 32
KEY_HEADS = 4
HEAD_WIDTH = 128
SPAN = 16
ADAPTER_SCALE = 0.5
NEG_LARGE = -1e30

STEP_ROWS = 16
HALF_ROWS = 8


def attend_kernel(lengths_ref, joins_ref, q_ref, d_ref, k_ref, v_ref, o_ref):
    positions = k_ref.shape[0] // STEP_ROWS
    per_group = QUERY_HEADS // KEY_HEADS
    keys = HALF_ROWS * positions
    rows = per_group * HALF_ROWS
    scale = 1.0 / math.sqrt(HEAD_WIDTH)
    row_request = lax.broadcasted_iota(jnp.int32, (rows, keys), 0) % HALF_ROWS
    column = lax.broadcasted_iota(jnp.int32, (rows, keys), 1)
    own = row_request == column // positions
    position = column % positions
    halves = []
    for half in range(2):
        limits = lengths_ref[0, half * HALF_ROWS : (half + 1) * HALF_ROWS, 0:1]
        joins = joins_ref[0, half * HALF_ROWS : (half + 1) * HALF_ROWS, 0:1]
        low = jnp.where(joins == 0, 0, limits - SPAN)
        limits = jnp.concatenate([limits] * per_group, axis=0)
        low = jnp.concatenate([low] * per_group, axis=0)
        visible = own & (position < limits) & (position >= low)
        outs = []
        for group in range(KEY_HEADS):
            lanes = pl.ds(group * HEAD_WIDTH, HEAD_WIDTH)
            key_block = k_ref[pl.ds(half * keys, keys), lanes]
            value_block = v_ref[pl.ds(half * keys, keys), lanes]
            pieces = []
            for ref in (q_ref, d_ref):
                for head in range(per_group):
                    at = (group * per_group + head) * HEAD_WIDTH
                    piece = ref[:, pl.ds(at, HEAD_WIDTH)].astype(jnp.float32)
                    pieces.append(piece[half * HALF_ROWS : (half + 1) * HALF_ROWS])
            queries = jnp.concatenate(pieces, axis=0).astype(jnp.bfloat16)
            both = lax.dot_general(
                queries, key_block, (((1,), (1,)), ((), ())), preferred_element_type=jnp.float32
            )
            scores = (both[:rows] + both[rows:]) * scale
            scores = jnp.where(visible, scores, NEG_LARGE)
            top = jnp.max(scores, axis=1, keepdims=True)
            raised = jnp.where(visible, jnp.exp(scores - top), 0.0)
            total = jnp.sum(raised, axis=1, keepdims=True)
            weights = (raised / total).astype(jnp.bfloat16)
            outs.append(jnp.dot(weights, value_block, preferred_element_type=jnp.float32))
        halves.append(outs)
    for group in range(KEY_HEADS):
        for head in range(per_group):
            at = (group * per_group + head) * HEAD_WIDTH
            span = slice(head * HALF_ROWS, (head + 1) * HALF_ROWS)
            tile = jnp.concatenate([halves[0][group][span], halves[1][group][span]], axis=0)
            o_ref[:, pl.ds(at, HEAD_WIDTH)] = tile.astype(o_ref.dtype)


def attend(base_queries, query_shift, keys, values, cache_lengths, joining_flags):
    rows, width = base_queries.shape
    positions, cache_width = keys.shape[1:]
    steps = rows // STEP_ROWS
    keys = keys.reshape(rows * positions, cache_width)
    values = values.reshape(rows * positions, cache_width)
    lengths = jnp.broadcast_to(cache_lengths.reshape(steps, STEP_ROWS, 1), (steps, STEP_ROWS, 128))
    joins = jnp.broadcast_to(joining_flags.reshape(steps, STEP_ROWS, 1), (steps, STEP_ROWS, 128))
    small = pl.BlockSpec((1, STEP_ROWS, 128), lambda i: (i, 0, 0))
    wide = pl.BlockSpec((STEP_ROWS, width), lambda i: (i, 0))
    cache = pl.BlockSpec((STEP_ROWS * positions, cache_width), lambda i: (i, 0))
    return pl.pallas_call(
        attend_kernel,
        grid=(steps,),
        in_specs=[small, small, wide, wide, cache, cache],
        out_specs=wide,
        out_shape=jax.ShapeDtypeStruct((rows, width), jnp.bfloat16),
        compiler_params=pltpu.CompilerParams(vmem_limit_bytes=32 * 1024 * 1024),
        cost_estimate=pl.CostEstimate(
            flops=2 * 3 * rows * positions * HALF_ROWS * width,
            bytes_accessed=2 * (keys.size + values.size + 3 * rows * width),
            transcendentals=rows * positions * QUERY_HEADS * HALF_ROWS,
        ),
    )(lengths, joins, base_queries, query_shift, keys, values)


def swapped(block, axis, bit):
    count = lax.axis_size(axis)
    route = []
    for low in range(count):
        high = low | 1 << bit
        if high != low and high < count:
            route += [(low, high), (high, low)]
    return lax.ppermute(block, axis, route)


def stores_of(adapter_index, adapter_owner_row):
    adapter_column = adapter_index[:, 0]
    table = jnp.arange(adapter_owner_row.shape[0], dtype=jnp.int32)
    return jnp.sum(
        jnp.where(adapter_column[:, None] == table[None, :], adapter_owner_row[None, :], 0), axis=1
    )


def routed_rows(hidden_state_rows, stores, down_factors, up_factors):
    replicas = lax.axis_size("replica")
    total_rows = hidden_state_rows.shape[0]
    capacity = max(2, (2 * total_rows + replicas - 1) // replicas)
    order = jnp.arange(total_rows, dtype=jnp.int32)
    earlier = (stores[:, None] == stores[None, :]) & (order[None, :] < order[:, None])
    slot_index = jnp.sum(earlier.astype(jnp.int32), axis=1)
    target = stores * capacity + slot_index
    slots = jnp.arange(replicas * capacity, dtype=jnp.int32)
    placing = (slots[:, None] == target[None, :]).astype(jnp.bfloat16)
    outgoing = jnp.dot(placing, hidden_state_rows, preferred_element_type=jnp.float32).astype(
        jnp.bfloat16
    )
    outgoing = outgoing.reshape(replicas, capacity, hidden_state_rows.shape[1])
    arrived = lax.all_to_all(outgoing, "replica", split_axis=0, concat_axis=0, tiled=True)
    sources = arrived.shape[0]
    items = arrived.shape[1]
    flat_rows = arrived.reshape(sources * items, arrived.shape[2])
    narrowed_rows = jnp.dot(flat_rows, down_factors[0], preferred_element_type=jnp.float32).astype(
        jnp.bfloat16
    )
    widened_rows = (
        ADAPTER_SCALE * jnp.dot(narrowed_rows, up_factors[0], preferred_element_type=jnp.float32)
    ).astype(jnp.bfloat16)
    computed = widened_rows.reshape(sources, items, widened_rows.shape[1])
    returned = lax.all_to_all(computed, "replica", split_axis=0, concat_axis=0, tiled=True)
    returned = returned.reshape(replicas * capacity, returned.shape[2])
    picked = jnp.einsum("sr,sq->rq", placing, returned, preferred_element_type=jnp.float32)
    return picked.astype(jnp.bfloat16)


def per_device(
    hidden_state_rows,
    base_queries,
    cached_key_rows,
    cached_value_rows,
    cache_lengths,
    joining_flags,
    adapter_index,
    adapter_owner_row,
    pair_trade_flags,
    down_factors,
    up_factors,
):
    here = lax.axis_index("replica")
    trade = lax.dynamic_index_in_dim(pair_trade_flags, here // 2, 0, keepdims=False) == 1
    stores = stores_of(adapter_index, adapter_owner_row)
    query_shift = routed_rows(hidden_state_rows, stores, down_factors, up_factors)
    attended = attend(
        base_queries,
        query_shift,
        cached_key_rows,
        cached_value_rows,
        cache_lengths,
        joining_flags,
    )
    return jnp.where(trade, swapped(attended, "replica", 0), attended)


def solution(mesh):
    placed = (
        P(("groups", "replica"), None),
        P(("groups", "replica"), None),
        P(("groups", "replica"), None, None),
        P(("groups", "replica"), None, None),
        P(("groups", "replica")),
        P(("groups", "replica")),
        P(("groups", "replica"), None),
        P(),
        P("groups"),
        P("replica", None, None),
        P("replica", None, None),
    )
    return jax.shard_map(
        per_device,
        mesh=mesh,
        in_specs=placed,
        out_specs=P(("groups", "replica"), None),
        check_vma=False,
    )
```

```python
import functools
import math

import jax
import jax.numpy as jnp
from jax import lax
from jax.experimental import pallas as pl
from jax.experimental.pallas import tpu as pltpu
from jax.sharding import PartitionSpec as P

QUERY_HEADS = 32
KEY_HEADS = 4
HEAD_WIDTH = 128
SPAN = 16
ADAPTER_SCALE = 0.5
ADAPTER_RANK = 64
NEG_LARGE = -1e30

STEP_ROWS = 16
HALF_ROWS = 8


def attend_kernel(lengths_ref, joins_ref, q_ref, d_ref, k_ref, v_ref, o_ref):
    positions = k_ref.shape[0] // STEP_ROWS
    per_group = QUERY_HEADS // KEY_HEADS
    keys = HALF_ROWS * positions
    rows = per_group * HALF_ROWS
    scale = 1.0 / math.sqrt(HEAD_WIDTH)
    row_request = lax.broadcasted_iota(jnp.int32, (rows, keys), 0) % HALF_ROWS
    column = lax.broadcasted_iota(jnp.int32, (rows, keys), 1)
    own = row_request == column // positions
    position = column % positions
    halves = []
    for half in range(2):
        limits = lengths_ref[0, half * HALF_ROWS : (half + 1) * HALF_ROWS, 0:1]
        joins = joins_ref[0, half * HALF_ROWS : (half + 1) * HALF_ROWS, 0:1]
        low = jnp.where(joins == 0, 0, limits - SPAN)
        limits = jnp.concatenate([limits] * per_group, axis=0)
        low = jnp.concatenate([low] * per_group, axis=0)
        visible = own & (position < limits) & (position >= low)
        outs = []
        for group in range(KEY_HEADS):
            lanes = pl.ds(group * HEAD_WIDTH, HEAD_WIDTH)
            key_block = k_ref[pl.ds(half * keys, keys), lanes]
            value_block = v_ref[pl.ds(half * keys, keys), lanes]
            pieces = []
            for ref in (q_ref, d_ref):
                for head in range(per_group):
                    at = (group * per_group + head) * HEAD_WIDTH
                    piece = ref[:, pl.ds(at, HEAD_WIDTH)].astype(jnp.float32)
                    pieces.append(piece[half * HALF_ROWS : (half + 1) * HALF_ROWS])
            queries = jnp.concatenate(pieces, axis=0).astype(jnp.bfloat16)
            both = lax.dot_general(
                queries, key_block, (((1,), (1,)), ((), ())), preferred_element_type=jnp.float32
            )
            scores = (both[:rows] + both[rows:]) * scale
            scores = jnp.where(visible, scores, NEG_LARGE)
            top = jnp.max(scores, axis=1, keepdims=True)
            raised = jnp.where(visible, jnp.exp(scores - top), 0.0)
            total = jnp.sum(raised, axis=1, keepdims=True)
            weights = (raised / total).astype(jnp.bfloat16)
            outs.append(jnp.dot(weights, value_block, preferred_element_type=jnp.float32))
        halves.append(outs)
    for group in range(KEY_HEADS):
        for head in range(per_group):
            at = (group * per_group + head) * HEAD_WIDTH
            span = slice(head * HALF_ROWS, (head + 1) * HALF_ROWS)
            tile = jnp.concatenate([halves[0][group][span], halves[1][group][span]], axis=0)
            o_ref[:, pl.ds(at, HEAD_WIDTH)] = tile.astype(o_ref.dtype)


def attend(base_queries, query_shift, keys, values, cache_lengths, joining_flags):
    rows, width = base_queries.shape
    positions, cache_width = keys.shape[1:]
    steps = rows // STEP_ROWS
    keys = keys.reshape(rows * positions, cache_width)
    values = values.reshape(rows * positions, cache_width)
    lengths = jnp.broadcast_to(cache_lengths.reshape(steps, STEP_ROWS, 1), (steps, STEP_ROWS, 128))
    joins = jnp.broadcast_to(joining_flags.reshape(steps, STEP_ROWS, 1), (steps, STEP_ROWS, 128))
    small = pl.BlockSpec((1, STEP_ROWS, 128), lambda i: (i, 0, 0))
    wide = pl.BlockSpec((STEP_ROWS, width), lambda i: (i, 0))
    cache = pl.BlockSpec((STEP_ROWS * positions, cache_width), lambda i: (i, 0))
    return pl.pallas_call(
        attend_kernel,
        grid=(steps,),
        in_specs=[small, small, wide, wide, cache, cache],
        out_specs=wide,
        out_shape=jax.ShapeDtypeStruct((rows, width), jnp.bfloat16),
        compiler_params=pltpu.CompilerParams(vmem_limit_bytes=32 * 1024 * 1024),
        cost_estimate=pl.CostEstimate(
            flops=2 * 3 * rows * positions * HALF_ROWS * width,
            bytes_accessed=2 * (keys.size + values.size + 3 * rows * width),
            transcendentals=rows * positions * QUERY_HEADS * HALF_ROWS,
        ),
    )(lengths, joins, base_queries, query_shift, keys, values)


def swapped(block, axis, bit):
    count = lax.axis_size(axis)
    route = []
    for low in range(count):
        high = low | 1 << bit
        if high != low and high < count:
            route += [(low, high), (high, low)]
    return lax.ppermute(block, axis, route)


def stores_of(adapter_index, adapter_owner_row):
    adapter_column = adapter_index[:, 0]
    table = jnp.arange(adapter_owner_row.shape[0], dtype=jnp.int32)
    return jnp.sum(
        jnp.where(adapter_column[:, None] == table[None, :], adapter_owner_row[None, :], 0), axis=1
    )

PLANE = 4
ROUTES = pl.DeviceIdType.MESH


def gathered_kernel(
    layers, h_ref, st_ref, down_ref, up_ref, out_ref,
    h_buf, st_buf, down_buf, up_buf, part, part_in, narrow, narrow_all, spread, wide,
    local_sem, h_send, h_recv, st_send, st_recv,
    down_send, down_recv, up_send, up_recv, climb_send, sink_send, climb_up_send, sink_up_send,
    part_send, part_recv, narrow_send, narrow_recv, wide_send, wide_recv,
):
    rows = h_ref.shape[0]
    rank, depth = ADAPTER_RANK, down_buf.shape[1]
    lanes = up_buf.shape[1]
    group, here = lax.axis_index("groups"), lax.axis_index("replica")
    layer, local = here // PLANE, here % PLANE
    side, core = local // 2, local % 2
    me = group * PLANE + local
    peers = 2 * PLANE

    def peer(i):
        g = (group + i // 4) % 2
        l = ((side + (i // 2) % 2) % 2) * 2 + (core + i % 2) % 2
        return g, l, g * PLANE + l

    def push(src, dst, send, recv, g, r):
        return pltpu.make_async_remote_copy(
            src_ref=src, dst_ref=dst, send_sem=send, recv_sem=recv,
            device_id=(g, r), device_id_type=ROUTES,
        )

    def over_peers(body):
        def step(i, carry):
            body(*peer(i))
            return carry

        lax.fori_loop(1, peers, step, 0)

    def over_locals(body, first=0):
        def step(i, carry):
            body(peer(i)[1])
            return carry

        lax.fori_loop(first, PLANE, step, 0)

    barrier = pltpu.get_barrier_semaphore()

    def greet(g, l, j):
        pl.semaphore_signal(
            barrier, inc=1, device_id=(g, layer * PLANE + l), device_id_type=ROUTES
        )

    over_peers(greet)

    @pl.when(layer < layers - 1)
    def _():
        pl.semaphore_signal(barrier, inc=1, device_id=(group, here + PLANE), device_id_type=ROUTES)

    @pl.when(layer > 0)
    def _():
        pl.semaphore_signal(barrier, inc=1, device_id=(group, here - PLANE), device_id_type=ROUTES)

    inner = (layer + layers - 1) // layers - (layer + 1) // layers
    pl.semaphore_wait(barrier, peers + inner)

    def stored(buf, a):
        return buf.at[pl.ds(a * rank, rank), :]

    def piece(ref, j, size):
        return ref.at[:, pl.ds(j * size, size)]

    def block(ref, j):
        return ref.at[pl.ds(j * rows, rows), :]

    mine = [
        pltpu.make_async_copy(piece(down_ref, me, depth), stored(down_buf, here), local_sem.at[0]),
        pltpu.make_async_copy(piece(up_ref, me, lanes), stored(up_buf, here), local_sem.at[1]),
        pltpu.make_async_copy(piece(h_ref, me, depth), block(h_buf, me), local_sem.at[2]),
        pltpu.make_async_copy(st_ref, block(st_buf, me), local_sem.at[3]),
    ]
    for copy in mine:
        copy.start()

    def down_copy(l):
        j = group * PLANE + l
        return push(
            piece(down_ref, j, depth), stored(down_buf, here),
            down_send.at[l], down_recv.at[here], group, layer * PLANE + l,
        )

    def up_copy(l):
        j = group * PLANE + l
        return push(
            piece(up_ref, j, lanes), stored(up_buf, here),
            up_send.at[l], up_recv.at[here], group, layer * PLANE + l,
        )

    def h_copy(g, l, j):
        return push(
            piece(h_ref, j, depth), block(h_buf, me),
            h_send.at[j], h_recv.at[me], g, layer * PLANE + l,
        )

    def st_copy(g, l, j):
        return push(
            st_ref, block(st_buf, me), st_send.at[j], st_recv.at[me], g, layer * PLANE + l
        )

    over_locals(lambda l: down_copy(l).start(), 1)
    mine[0].wait()
    mine[1].wait()

    def onward(buf, a, send, recv, step):
        return push(
            stored(buf, a), stored(buf, a), send.at[a], recv.at[a], group, here + step * PLANE
        )

    def arrived(buf, a, recv):
        push(stored(buf, a), stored(buf, a), local_sem.at[4], recv.at[a], group, here).wait_recv()

    def first_hop(buf, recv, climb, sink, l):
        a = layer * PLANE + l

        @pl.when(l != local)
        def _():
            arrived(buf, a, recv)

        @pl.when(layer < layers - 1)
        def _():
            onward(buf, a, climb, recv, 1).start()

        @pl.when(layer > 0)
        def _():
            onward(buf, a, sink, recv, -1).start()

    def later_hop(buf, recv, climb, sink, t, l):
        @pl.when(layer - t >= 0)
        def _():
            a = (layer - t) * PLANE + l
            arrived(buf, a, recv)

            @pl.when(layer < layers - 1)
            def _():
                onward(buf, a, climb, recv, 1).start()

        @pl.when(layer + t < layers)
        def _():
            a = (layer + t) * PLANE + l
            arrived(buf, a, recv)

            @pl.when(layer > 0)
            def _():
                onward(buf, a, sink, recv, -1).start()

    downs = (down_buf, down_recv, climb_send, sink_send)
    ups = (up_buf, up_recv, climb_up_send, sink_up_send)
    first_hop(*downs, local)
    over_peers(lambda g, l, j: st_copy(g, l, j).start())
    over_locals(lambda l: first_hop(*downs, l), 1)
    over_peers(lambda g, l, j: h_copy(g, l, j).start())
    over_locals(lambda l: up_copy(l).start(), 1)
    for t in range(1, layers - 1):
        over_locals(lambda l: later_hop(*downs, t, l))
    over_locals(lambda l: first_hop(*ups, l))
    mine[2].wait()
    mine[3].wait()

    def here_recv(src, dst, recv, g, l):
        push(src, dst, local_sem.at[4], recv, g, layer * PLANE + l).wait_recv()

    over_peers(lambda g, l, j: here_recv(block(h_buf, j), block(h_buf, j), h_recv.at[j], g, l))
    over_peers(lambda g, l, j: here_recv(block(st_buf, j), block(st_buf, j), st_recv.at[j], g, l))
    over_locals(lambda l: later_hop(*downs, layers - 1, l))

    lane = lax.broadcasted_iota(jnp.int32, (1, 2 * rank), 1) // rank
    part[...] = jnp.zeros_like(part)

    def narrowed(s, carry):
        at = pl.ds(s * 4 * rank, 4 * rank)
        both = lax.dot_general(
            h_buf[...], down_buf[at, :], (((1,), (1,)), ((), ())),
            preferred_element_type=jnp.float32,
        )
        stores = st_buf[...]
        kept = jnp.where(stores == s * 4 + lane, both[:, : 2 * rank], 0.0)
        kept = kept + jnp.where(stores == s * 4 + 2 + lane, both[:, 2 * rank :], 0.0)
        part[...] += kept
        return carry

    lax.fori_loop(0, down_buf.shape[0] // (4 * rank), narrowed, 0)

    def part_copy(g, l, j):
        return push(
            block(part, j), part_in.at[me], part_send.at[j], part_recv.at[me],
            g, layer * PLANE + l,
        )

    over_peers(lambda g, l, j: part_copy(g, l, j).start())
    for t in range(1, layers - 1):
        over_locals(lambda l: later_hop(*ups, t, l))
    over_peers(lambda g, l, j: here_recv(part_in.at[j], part_in.at[j], part_recv.at[j], g, l))
    part_in[me] = part[pl.ds(me * rows, rows), :]
    total = part_in[0]
    for j in range(1, peers):
        total = total + part_in[j]
    total = total + pltpu.roll(total, rank, 1)
    narrow[...] = total.astype(jnp.bfloat16)

    def narrow_copy(g, l, j):
        return push(
            narrow, block(narrow_all, me), narrow_send.at[j], narrow_recv.at[me],
            g, layer * PLANE + l,
        )

    over_peers(lambda g, l, j: narrow_copy(g, l, j).start())
    narrow_all[pl.ds(me * rows, rows), :] = narrow[...]
    over_peers(
        lambda g, l, j: here_recv(block(narrow_all, j), block(narrow_all, j), narrow_recv.at[j], g, l)
    )
    for s in range(spread.shape[1] // (2 * rank)):
        spread[:, s * 2 * rank : (s + 1) * 2 * rank] = jnp.where(
            st_buf[...] == 2 * s + lane, narrow_all[...].astype(jnp.float32), 0.0
        ).astype(jnp.bfloat16)
    over_locals(lambda l: later_hop(*ups, layers - 1, l))

    def widened(c, carry):
        at = pl.ds(c * 256, 256)
        block_of = jnp.dot(spread[...], up_buf[:, at], preferred_element_type=jnp.float32)
        wide[:, at] = (ADAPTER_SCALE * block_of).astype(jnp.bfloat16)
        return carry

    lax.fori_loop(0, lanes // 256, widened, 0)

    def wide_copy(g, l, j):
        return push(
            block(wide, j), piece(out_ref, me, lanes), wide_send.at[j], wide_recv.at[me],
            g, layer * PLANE + l,
        )

    over_peers(lambda g, l, j: wide_copy(g, l, j).start())
    last = pltpu.make_async_copy(block(wide, me), piece(out_ref, me, lanes), local_sem.at[5])
    last.start()
    last.wait()
    over_peers(
        lambda g, l, j: here_recv(
            piece(out_ref, j, lanes), piece(out_ref, j, lanes), wide_recv.at[j], g, l
        )
    )

    def left(l):
        down_copy(l).wait_send()
        up_copy(l).wait_send()

    over_locals(left, 1)

    def left_peer(g, l, j):
        h_copy(g, l, j).wait_send()
        st_copy(g, l, j).wait_send()
        part_copy(g, l, j).wait_send()
        narrow_copy(g, l, j).wait_send()
        wide_copy(g, l, j).wait_send()

    over_peers(left_peer)

    def passed(s, carry):
        def one(l):
            a = s * PLANE + l

            @pl.when((layer < layers - 1) & (s <= layer))
            def _():
                onward(down_buf, a, climb_send, down_recv, 1).wait_send()
                onward(up_buf, a, climb_up_send, up_recv, 1).wait_send()

            @pl.when((layer > 0) & (s >= layer))
            def _():
                onward(down_buf, a, sink_send, down_recv, -1).wait_send()
                onward(up_buf, a, sink_up_send, up_recv, -1).wait_send()

        over_locals(one)
        return carry

    lax.fori_loop(0, layers, passed, 0)


def gathered_rows(hidden_state_rows, stores, down_factors, up_factors):
    replicas = lax.axis_size("replica")
    rows, depth = hidden_state_rows.shape
    rank, width = up_factors.shape[1:]
    layers = replicas // PLANE
    peers = 2 * PLANE
    down = jnp.swapaxes(down_factors[0], 0, 1)
    tags = jnp.broadcast_to(stores[:, None], (rows, 128))
    dma = pltpu.SemaphoreType.DMA
    here = pl.BlockSpec(memory_space=pltpu.VMEM)
    return pl.pallas_call(
        functools.partial(gathered_kernel, layers),
        in_specs=[here] * 4,
        out_specs=pl.BlockSpec(memory_space=pl.ANY),
        out_shape=jax.ShapeDtypeStruct((rows, width), jnp.bfloat16),
        scratch_shapes=[
            pltpu.VMEM((peers * rows, depth // peers), jnp.bfloat16),
            pltpu.VMEM((peers * rows, 128), jnp.int32),
            pltpu.VMEM((replicas * rank, depth // peers), jnp.bfloat16),
            pltpu.VMEM((replicas * rank, width // peers), jnp.bfloat16),
            pltpu.VMEM((peers * rows, 128), jnp.float32),
            pltpu.VMEM((peers, rows, 128), jnp.float32),
            pltpu.VMEM((rows, 128), jnp.bfloat16),
            pltpu.VMEM((peers * rows, 128), jnp.bfloat16),
            pltpu.VMEM((peers * rows, replicas * rank), jnp.bfloat16),
            pltpu.VMEM((peers * rows, width // peers), jnp.bfloat16),
            dma((6,)),
            dma((peers,)), dma((peers,)), dma((peers,)), dma((peers,)),
            dma((PLANE,)), dma((replicas,)), dma((PLANE,)), dma((replicas,)),
            dma((replicas,)), dma((replicas,)), dma((replicas,)), dma((replicas,)),
            dma((peers,)), dma((peers,)), dma((peers,)), dma((peers,)),
            dma((peers,)), dma((peers,)),
        ],
        compiler_params=pltpu.CompilerParams(
            collective_id=0, has_side_effects=True, vmem_limit_bytes=40 * 1024 * 1024
        ),
        cost_estimate=pl.CostEstimate(
            flops=2 * peers * rows * replicas * rank * (depth + width) // peers,
            bytes_accessed=2 * rows * (depth + width) + 2 * rank * (depth + width),
            transcendentals=0,
        ),
    )(hidden_state_rows, tags, down, up_factors[0])


def routed_rows(hidden_state_rows, stores, down_factors, up_factors):
    replicas = lax.axis_size("replica")
    total_rows = hidden_state_rows.shape[0]
    capacity = max(2, (2 * total_rows + replicas - 1) // replicas)
    order = jnp.arange(total_rows, dtype=jnp.int32)
    earlier = (stores[:, None] == stores[None, :]) & (order[None, :] < order[:, None])
    slot_index = jnp.sum(earlier.astype(jnp.int32), axis=1)
    target = stores * capacity + slot_index
    slots = jnp.arange(replicas * capacity, dtype=jnp.int32)
    placing = (slots[:, None] == target[None, :]).astype(jnp.bfloat16)
    outgoing = jnp.dot(placing, hidden_state_rows, preferred_element_type=jnp.float32).astype(
        jnp.bfloat16
    )
    outgoing = outgoing.reshape(replicas, capacity, hidden_state_rows.shape[1])
    arrived = lax.all_to_all(outgoing, "replica", split_axis=0, concat_axis=0, tiled=True)
    sources = arrived.shape[0]
    items = arrived.shape[1]
    flat_rows = arrived.reshape(sources * items, arrived.shape[2])
    narrowed_rows = jnp.dot(flat_rows, down_factors[0], preferred_element_type=jnp.float32).astype(
        jnp.bfloat16
    )
    widened_rows = (
        ADAPTER_SCALE * jnp.dot(narrowed_rows, up_factors[0], preferred_element_type=jnp.float32)
    ).astype(jnp.bfloat16)
    computed = widened_rows.reshape(sources, items, widened_rows.shape[1])
    returned = lax.all_to_all(computed, "replica", split_axis=0, concat_axis=0, tiled=True)
    returned = returned.reshape(replicas * capacity, returned.shape[2])
    picked = jnp.einsum("sr,sq->rq", placing, returned, preferred_element_type=jnp.float32)
    return picked.astype(jnp.bfloat16)


def per_device(
    hidden_state_rows,
    base_queries,
    cached_key_rows,
    cached_value_rows,
    cache_lengths,
    joining_flags,
    adapter_index,
    adapter_owner_row,
    pair_trade_flags,
    down_factors,
    up_factors,
):
    here = lax.axis_index("replica")
    trade = lax.dynamic_index_in_dim(pair_trade_flags, here // 2, 0, keepdims=False) == 1
    stores = stores_of(adapter_index, adapter_owner_row)
    few = lax.axis_size("replica") == 4 * PLANE and lax.axis_size("groups") == 2
    shifted = gathered_rows if few else routed_rows
    query_shift = shifted(hidden_state_rows, stores, down_factors, up_factors)
    attended = attend(
        base_queries,
        query_shift,
        cached_key_rows,
        cached_value_rows,
        cache_lengths,
        joining_flags,
    )
    return jnp.where(trade, swapped(attended, "replica", 0), attended)


def solution(mesh):
    placed = (
        P(("groups", "replica"), None),
        P(("groups", "replica"), None),
        P(("groups", "replica"), None, None),
        P(("groups", "replica"), None, None),
        P(("groups", "replica")),
        P(("groups", "replica")),
        P(("groups", "replica"), None),
        P(),
        P("groups"),
        P("replica", None, None),
        P("replica", None, None),
    )
    return jax.shard_map(
        per_device,
        mesh=mesh,
        in_specs=placed,
        out_specs=P(("groups", "replica"), None),
        check_vma=False,
    )
```

```python
import functools
import math

import jax
import jax.numpy as jnp
from jax import lax
from jax.experimental import pallas as pl
from jax.experimental.pallas import tpu as pltpu
from jax.sharding import PartitionSpec as P

QUERY_HEADS = 32
KEY_HEADS = 4
HEAD_WIDTH = 128
SPAN = 16
ADAPTER_SCALE = 0.5
ADAPTER_RANK = 64
NEG_LARGE = -1e30

STEP_ROWS = 16
HALF_ROWS = 8


def attend_kernel(lengths_ref, joins_ref, q_ref, d_ref, k_ref, v_ref, o_ref):
    positions = k_ref.shape[0] // STEP_ROWS
    per_group = QUERY_HEADS // KEY_HEADS
    keys = HALF_ROWS * positions
    rows = per_group * HALF_ROWS
    scale = 1.0 / math.sqrt(HEAD_WIDTH)
    row_request = lax.broadcasted_iota(jnp.int32, (rows, keys), 0) % HALF_ROWS
    column = lax.broadcasted_iota(jnp.int32, (rows, keys), 1)
    own = row_request == column // positions
    position = column % positions
    halves = []
    for half in range(2):
        limits = lengths_ref[0, half * HALF_ROWS : (half + 1) * HALF_ROWS, 0:1]
        joins = joins_ref[0, half * HALF_ROWS : (half + 1) * HALF_ROWS, 0:1]
        low = jnp.where(joins == 0, 0, limits - SPAN)
        limits = jnp.concatenate([limits] * per_group, axis=0)
        low = jnp.concatenate([low] * per_group, axis=0)
        visible = own & (position < limits) & (position >= low)
        outs = []
        for group in range(KEY_HEADS):
            lanes = pl.ds(group * HEAD_WIDTH, HEAD_WIDTH)
            key_block = k_ref[pl.ds(half * keys, keys), lanes]
            value_block = v_ref[pl.ds(half * keys, keys), lanes]
            pieces = []
            for ref in (q_ref, d_ref):
                for head in range(per_group):
                    at = (group * per_group + head) * HEAD_WIDTH
                    piece = ref[:, pl.ds(at, HEAD_WIDTH)].astype(jnp.float32)
                    pieces.append(piece[half * HALF_ROWS : (half + 1) * HALF_ROWS])
            queries = jnp.concatenate(pieces, axis=0).astype(jnp.bfloat16)
            both = lax.dot_general(
                queries, key_block, (((1,), (1,)), ((), ())), preferred_element_type=jnp.float32
            )
            scores = (both[:rows] + both[rows:]) * scale
            scores = jnp.where(visible, scores, NEG_LARGE)
            top = jnp.max(scores, axis=1, keepdims=True)
            raised = jnp.where(visible, jnp.exp(scores - top), 0.0)
            total = jnp.sum(raised, axis=1, keepdims=True)
            weights = (raised / total).astype(jnp.bfloat16)
            outs.append(jnp.dot(weights, value_block, preferred_element_type=jnp.float32))
        halves.append(outs)
    for group in range(KEY_HEADS):
        for head in range(per_group):
            at = (group * per_group + head) * HEAD_WIDTH
            span = slice(head * HALF_ROWS, (head + 1) * HALF_ROWS)
            tile = jnp.concatenate([halves[0][group][span], halves[1][group][span]], axis=0)
            o_ref[:, pl.ds(at, HEAD_WIDTH)] = tile.astype(o_ref.dtype)


def attend(base_queries, query_shift, keys, values, cache_lengths, joining_flags):
    rows, width = base_queries.shape
    positions, cache_width = keys.shape[1:]
    steps = rows // STEP_ROWS
    keys = keys.reshape(rows * positions, cache_width)
    values = values.reshape(rows * positions, cache_width)
    lengths = jnp.broadcast_to(cache_lengths.reshape(steps, STEP_ROWS, 1), (steps, STEP_ROWS, 128))
    joins = jnp.broadcast_to(joining_flags.reshape(steps, STEP_ROWS, 1), (steps, STEP_ROWS, 128))
    small = pl.BlockSpec((1, STEP_ROWS, 128), lambda i: (i, 0, 0))
    wide = pl.BlockSpec((STEP_ROWS, width), lambda i: (i, 0))
    cache = pl.BlockSpec((STEP_ROWS * positions, cache_width), lambda i: (i, 0))
    return pl.pallas_call(
        attend_kernel,
        grid=(steps,),
        in_specs=[small, small, wide, wide, cache, cache],
        out_specs=wide,
        out_shape=jax.ShapeDtypeStruct((rows, width), jnp.bfloat16),
        compiler_params=pltpu.CompilerParams(vmem_limit_bytes=32 * 1024 * 1024),
        cost_estimate=pl.CostEstimate(
            flops=2 * 3 * rows * positions * HALF_ROWS * width,
            bytes_accessed=2 * (keys.size + values.size + 3 * rows * width),
            transcendentals=rows * positions * QUERY_HEADS * HALF_ROWS,
        ),
    )(lengths, joins, base_queries, query_shift, keys, values)


def swapped(block, axis, bit):
    count = lax.axis_size(axis)
    route = []
    for low in range(count):
        high = low | 1 << bit
        if high != low and high < count:
            route += [(low, high), (high, low)]
    return lax.ppermute(block, axis, route)


def stores_of(adapter_index, adapter_owner_row):
    adapter_column = adapter_index[:, 0]
    table = jnp.arange(adapter_owner_row.shape[0], dtype=jnp.int32)
    return jnp.sum(
        jnp.where(adapter_column[:, None] == table[None, :], adapter_owner_row[None, :], 0), axis=1
    )

PLANE = 4
ROUTES = pl.DeviceIdType.MESH


def gathered_kernel(
    layers, h_ref, st_ref, down_ref, up_ref, out_ref,
    h_buf, far_buf, st_buf, far_st, tags, far_tags, down_buf, up_buf, part, packed, far_packed, part_in, total_ref, narrow, narrow_all, spread, wide,
    local_sem, h_send, h_recv, st_send, st_recv,
    far_send, far_recv, far_st_send, far_st_recv, far_part_send, far_part_recv,
    down_send, down_recv, up_send, up_recv, climb_send, sink_send, climb_up_send, sink_up_send,
    part_send, part_recv, narrow_send, narrow_recv, wide_send, wide_recv,
):
    rows = h_ref.shape[0]
    rank, depth = ADAPTER_RANK, down_buf.shape[1]
    lanes = up_buf.shape[1]
    group, here = lax.axis_index("groups"), lax.axis_index("replica")
    layer, local = here // PLANE, here % PLANE
    side, core = local // 2, local % 2
    me = group * PLANE + local
    peers = 2 * PLANE
    half, packs = depth // 2, rows // 2
    partner = layer + 1 - 2 * (layer % 2)
    end = (layer == 0) | (layer == layers - 1)
    inside = (layer > 0) & (layer < layers - 1)

    def peer(i):
        g = (group + i // 4) % 2
        l = ((side + (i // 2) % 2) % 2) * 2 + (core + i % 2) % 2
        return g, l, g * PLANE + l

    def push(src, dst, send, recv, g, r):
        return pltpu.make_async_remote_copy(
            src_ref=src, dst_ref=dst, send_sem=send, recv_sem=recv,
            device_id=(g, r), device_id_type=ROUTES,
        )

    def over_peers(body):
        def step(i, carry):
            body(*peer(i))
            return carry

        lax.fori_loop(1, peers, step, 0)

    def over_all(body):
        def step(i, carry):
            body(*peer(i))
            return carry

        lax.fori_loop(0, peers, step, 0)

    def over_locals(body, first=0):
        def step(i, carry):
            body(peer(i)[1])
            return carry

        lax.fori_loop(first, PLANE, step, 0)

    barrier = pltpu.get_barrier_semaphore()

    def greet(g, l, j):
        pl.semaphore_signal(
            barrier, inc=1, device_id=(g, layer * PLANE + l), device_id_type=ROUTES
        )

    over_peers(greet)

    def greet_far(g, l, j):
        pl.semaphore_signal(
            barrier, inc=1, device_id=(g, partner * PLANE + l), device_id_type=ROUTES
        )

    over_all(greet_far)

    @pl.when(inside)
    def _():
        other = (2 * layer - partner) * PLANE + local
        pl.semaphore_signal(barrier, inc=1, device_id=(group, other), device_id_type=ROUTES)

    inner = (layer + layers - 1) // layers - (layer + 1) // layers
    pl.semaphore_wait(barrier, 2 * peers - 1 + inner)

    def stored(buf, a):
        return buf.at[pl.ds(a * rank, rank), :]

    def stored_half(buf, a):
        return buf.at[pl.ds(a * rank, rank), pl.ds(0, half)]

    def left_half(ref, j):
        return ref.at[:, pl.ds(j * depth, half)]

    def right_half(ref, j):
        return ref.at[:, pl.ds(j * depth + half, half)]

    def near_half(j):
        return h_buf.at[pl.ds(j * rows, rows), pl.ds(0, half)]

    def tag_rows(ref, j):
        return ref.at[pl.ds(j * 8, 8), :]

    def piece(ref, j, size):
        return ref.at[:, pl.ds(j * size, size)]

    def block(ref, j):
        return ref.at[pl.ds(j * rows, rows), :]

    mine = [
        pltpu.make_async_copy(piece(down_ref, me, depth), stored(down_buf, here), local_sem.at[0]),
        pltpu.make_async_copy(piece(up_ref, me, lanes), stored(up_buf, here), local_sem.at[1]),
        pltpu.make_async_copy(piece(h_ref, me, depth), block(h_buf, me), local_sem.at[2]),
        pltpu.make_async_copy(st_ref, tag_rows(st_buf, me), local_sem.at[3]),
    ]
    for copy in mine:
        copy.start()

    def down_copy(l):
        j = group * PLANE + l
        return push(
            piece(down_ref, j, depth), stored(down_buf, here),
            down_send.at[l], down_recv.at[here], group, layer * PLANE + l,
        )

    def up_copy(l):
        j = group * PLANE + l
        return push(
            piece(up_ref, j, lanes), stored(up_buf, here),
            up_send.at[l], up_recv.at[here], group, layer * PLANE + l,
        )

    def h_copy(g, l, j):
        return push(
            piece(h_ref, j, depth), block(h_buf, me),
            h_send.at[j], h_recv.at[me], g, layer * PLANE + l,
        )

    def h_half(g, l, j):
        return push(
            left_half(h_ref, j), near_half(me), h_send.at[j], h_recv.at[me], g, layer * PLANE + l
        )

    def far_copy(g, l, j):
        return push(
            right_half(h_ref, j), block(far_buf, me), far_send.at[j], far_recv.at[me],
            g, partner * PLANE + l,
        )

    def st_copy(g, l, j):
        return push(
            st_ref, tag_rows(st_buf, me), st_send.at[j], st_recv.at[me], g, layer * PLANE + l
        )

    def far_st_copy(g, l, j):
        return push(
            st_ref, tag_rows(far_st, me), far_st_send.at[j], far_st_recv.at[me],
            g, partner * PLANE + l,
        )

    over_locals(lambda l: down_copy(l).start(), 1)
    mine[0].wait()
    mine[1].wait()

    def onward(buf, a, send, recv, step, view):
        return push(
            view(buf, a), view(buf, a), send.at[a], recv.at[a], group, here + step * PLANE
        )

    def arrived(buf, a, recv, view):
        push(view(buf, a), view(buf, a), local_sem.at[4], recv.at[a], group, here).wait_recv()

    def hop(buf, a, send, recv, step, split, do):
        if not split:
            do(onward(buf, a, send, recv, step, stored))
            return
        to_end = layer == (layers - 2 if step > 0 else 1)

        @pl.when(to_end)
        def _():
            do(onward(buf, a, send, recv, step, stored_half))

        @pl.when(jnp.logical_not(to_end))
        def _():
            do(onward(buf, a, send, recv, step, stored))

    def start(copy):
        copy.start()

    def first_hop(buf, recv, climb, sink, split, l):
        a = layer * PLANE + l

        @pl.when(l != local)
        def _():
            arrived(buf, a, recv, stored)

        @pl.when(layer < layers - 1)
        def _():
            hop(buf, a, climb, recv, 1, split, start)

        @pl.when(layer > 0)
        def _():
            hop(buf, a, sink, recv, -1, split, start)

    def landed(buf, a, recv, split):
        if not split:
            arrived(buf, a, recv, stored)
            return

        @pl.when(end)
        def _():
            arrived(buf, a, recv, stored_half)

        @pl.when(inside)
        def _():
            arrived(buf, a, recv, stored)

    def later_hop(buf, recv, climb, sink, split, t, l):
        @pl.when(layer - t >= 0)
        def _():
            a = (layer - t) * PLANE + l
            landed(buf, a, recv, split)

            @pl.when(layer < layers - 1)
            def _():
                hop(buf, a, climb, recv, 1, split, start)

        @pl.when(layer + t < layers)
        def _():
            a = (layer + t) * PLANE + l
            landed(buf, a, recv, split)

            @pl.when(layer > 0)
            def _():
                hop(buf, a, sink, recv, -1, split, start)

    downs = (down_buf, down_recv, climb_send, sink_send, True)
    ups = (up_buf, up_recv, climb_up_send, sink_up_send, False)
    first_hop(*downs, local)
    over_peers(lambda g, l, j: st_copy(g, l, j).start())
    over_locals(lambda l: first_hop(*downs, l), 1)

    @pl.when(end)
    def _():
        over_all(lambda g, l, j: far_st_copy(g, l, j).start())
        over_all(lambda g, l, j: far_copy(g, l, j).start())
        over_peers(lambda g, l, j: h_half(g, l, j).start())

    @pl.when(inside)
    def _():
        over_peers(lambda g, l, j: h_copy(g, l, j).start())

    over_locals(lambda l: up_copy(l).start(), 1)
    for t in range(1, layers - 1):
        over_locals(lambda l: later_hop(*downs, t, l))
    over_locals(lambda l: first_hop(*ups, l))
    mine[2].wait()
    mine[3].wait()

    def here_recv(src, dst, recv, g, l):
        push(src, dst, local_sem.at[4], recv, g, layer * PLANE + l).wait_recv()

    def taken(view, recv):
        return lambda g, l, j: here_recv(view(j), view(j), recv.at[j], g, l)

    def tagged(src, dst):
        for j in range(peers):
            row = src[j * 8 : j * 8 + 1, :].astype(jnp.float32)
            turned = jnp.transpose(jnp.broadcast_to(row, (128, 128)))
            dst[j * rows : (j + 1) * rows, :] = turned[:rows].astype(jnp.int32)

    over_peers(taken(lambda j: tag_rows(st_buf, j), st_recv))
    tagged(st_buf, tags)

    @pl.when(end)
    def _():
        over_peers(taken(near_half, h_recv))

    @pl.when(inside)
    def _():
        over_peers(taken(lambda j: block(h_buf, j), h_recv))
        over_all(taken(lambda j: tag_rows(far_st, j), far_st_recv))
        tagged(far_st, far_tags)

    over_locals(lambda l: later_hop(*downs, layers - 1, l))

    lane = lax.broadcasted_iota(jnp.int32, (1, 2 * rank), 1) // rank

    def products(left, right, stores_ref, to):
        part[...] = jnp.zeros_like(part)

        def narrowed(s, carry):
            at = pl.ds(s * 4 * rank, 4 * rank)
            both = lax.dot_general(
                left[...], right[at, :], (((1,), (1,)), ((), ())),
                preferred_element_type=jnp.float32,
            )
            stores = stores_ref[...]
            kept = jnp.where(stores == s * 4 + lane, both[:, : 2 * rank], 0.0)
            kept = kept + jnp.where(stores == s * 4 + 2 + lane, both[:, 2 * rank :], 0.0)
            part[...] += kept
            return carry

        lax.fori_loop(0, down_buf.shape[0] // (4 * rank), narrowed, 0)
        summed = part[...]
        summed = summed + pltpu.roll(summed, rank, 1)
        for j in range(peers):
            first = summed[j * rows : j * rows + packs]
            second = summed[j * rows + packs : (j + 1) * rows]
            to[j * packs : (j + 1) * packs, :] = jnp.where(lane == 0, first, second)

    def packs_of(ref, j):
        return ref.at[pl.ds(j * packs, packs), :]

    def part_copy(g, l, j):
        return push(
            packs_of(packed, j), part_in.at[me], part_send.at[j], part_recv.at[me],
            g, layer * PLANE + l,
        )

    def far_part_copy(g, l, j):
        return push(
            packs_of(far_packed, j), part_in.at[peers + me],
            far_part_send.at[j], far_part_recv.at[me], g, partner * PLANE + l,
        )

    @pl.when(end)
    def _():
        products(h_buf.at[:, pl.ds(0, half)], down_buf.at[:, pl.ds(0, half)], tags, packed)

    @pl.when(inside)
    def _():
        over_all(taken(lambda j: block(far_buf, j), far_recv))
        products(far_buf, down_buf.at[:, pl.ds(half, half)], far_tags, far_packed)
        over_all(lambda g, l, j: far_part_copy(g, l, j).start())
        products(h_buf, down_buf, tags, packed)

    over_peers(lambda g, l, j: part_copy(g, l, j).start())
    for t in range(1, layers - 1):
        over_locals(lambda l: later_hop(*ups, t, l))
    over_peers(taken(lambda j: part_in.at[j], part_recv))
    part_in[me] = packed[pl.ds(me * packs, packs), :]
    total = part_in[0]
    for j in range(1, peers):
        total = total + part_in[j]
    total_ref[...] = total

    @pl.when(end)
    def _():
        over_all(taken(lambda j: part_in.at[peers + j], far_part_recv))
        more = total_ref[...]
        for j in range(peers):
            more = more + part_in[peers + j]
        total_ref[...] = more

    narrow[...] = total_ref[...].astype(jnp.bfloat16)

    def narrow_copy(g, l, j):
        return push(
            narrow, packs_of(narrow_all, me), narrow_send.at[j], narrow_recv.at[me],
            g, layer * PLANE + l,
        )

    over_peers(lambda g, l, j: narrow_copy(g, l, j).start())
    narrow_all[pl.ds(me * packs, packs), :] = narrow[...]
    over_peers(taken(lambda j: packs_of(narrow_all, j), narrow_recv))
    for j in range(peers):
        pair = narrow_all[j * packs : (j + 1) * packs, :].astype(jnp.float32)
        turned = pltpu.roll(pair, rank, 1)
        own = jnp.concatenate(
            [jnp.where(lane == 0, pair, turned), jnp.where(lane == 0, turned, pair)], axis=0
        )
        stores = tags[j * rows : (j + 1) * rows, :]
        for s in range(spread.shape[1] // (2 * rank)):
            spread[j * rows : (j + 1) * rows, s * 2 * rank : (s + 1) * 2 * rank] = jnp.where(
                stores == 2 * s + lane, own, 0.0
            ).astype(jnp.bfloat16)
    over_locals(lambda l: later_hop(*ups, layers - 1, l))

    def widened(c, carry):
        at = pl.ds(c * 256, 256)
        block_of = jnp.dot(spread[...], up_buf[:, at], preferred_element_type=jnp.float32)
        wide[:, at] = (ADAPTER_SCALE * block_of).astype(jnp.bfloat16)
        return carry

    lax.fori_loop(0, lanes // 256, widened, 0)

    def wide_copy(g, l, j):
        return push(
            block(wide, j), piece(out_ref, me, lanes), wide_send.at[j], wide_recv.at[me],
            g, layer * PLANE + l,
        )

    over_peers(lambda g, l, j: wide_copy(g, l, j).start())
    last = pltpu.make_async_copy(block(wide, me), piece(out_ref, me, lanes), local_sem.at[5])
    last.start()
    last.wait()
    over_peers(
        lambda g, l, j: here_recv(
            piece(out_ref, j, lanes), piece(out_ref, j, lanes), wide_recv.at[j], g, l
        )
    )

    def left(l):
        down_copy(l).wait_send()
        up_copy(l).wait_send()

    over_locals(left, 1)

    def left_peer(g, l, j):
        st_copy(g, l, j).wait_send()
        part_copy(g, l, j).wait_send()
        narrow_copy(g, l, j).wait_send()
        wide_copy(g, l, j).wait_send()

    over_peers(left_peer)

    def left_far(g, l, j):
        far_st_copy(g, l, j).wait_send()
        far_copy(g, l, j).wait_send()

    @pl.when(end)
    def _():
        over_peers(lambda g, l, j: h_half(g, l, j).wait_send())
        over_all(left_far)

    @pl.when(inside)
    def _():
        over_peers(lambda g, l, j: h_copy(g, l, j).wait_send())
        over_all(lambda g, l, j: far_part_copy(g, l, j).wait_send())

    def sent(copy):
        copy.wait_send()

    def passed(s, carry):
        def one(l):
            a = s * PLANE + l

            @pl.when((layer < layers - 1) & (s <= layer))
            def _():
                hop(down_buf, a, climb_send, down_recv, 1, True, sent)
                hop(up_buf, a, climb_up_send, up_recv, 1, False, sent)

            @pl.when((layer > 0) & (s >= layer))
            def _():
                hop(down_buf, a, sink_send, down_recv, -1, True, sent)
                hop(up_buf, a, sink_up_send, up_recv, -1, False, sent)

        over_locals(one)
        return carry

    lax.fori_loop(0, layers, passed, 0)


def gathered_rows(hidden_state_rows, stores, down_factors, up_factors):
    replicas = lax.axis_size("replica")
    rows, depth = hidden_state_rows.shape
    rank, width = up_factors.shape[1:]
    layers = replicas // PLANE
    peers = 2 * PLANE
    down = jnp.swapaxes(down_factors[0], 0, 1)
    tags = jnp.broadcast_to(jnp.pad(stores, (0, 128 - rows))[None, :], (8, 128))
    dma = pltpu.SemaphoreType.DMA
    here = pl.BlockSpec(memory_space=pltpu.VMEM)
    far = pl.BlockSpec(memory_space=pl.ANY)
    return pl.pallas_call(
        functools.partial(gathered_kernel, layers),
        in_specs=[far, here, far, far],
        out_specs=pl.BlockSpec(memory_space=pl.ANY),
        out_shape=jax.ShapeDtypeStruct((rows, width), jnp.bfloat16),
        scratch_shapes=[
            pltpu.VMEM((peers * rows, depth // peers), jnp.bfloat16),
            pltpu.VMEM((peers * rows, depth // peers // 2), jnp.bfloat16),
            pltpu.VMEM((peers * 8, 128), jnp.int32),
            pltpu.VMEM((peers * 8, 128), jnp.int32),
            pltpu.VMEM((peers * rows, 128), jnp.int32),
            pltpu.VMEM((peers * rows, 128), jnp.int32),
            pltpu.VMEM((replicas * rank, depth // peers), jnp.bfloat16),
            pltpu.VMEM((replicas * rank, width // peers), jnp.bfloat16),
            pltpu.VMEM((peers * rows, 128), jnp.float32),
            pltpu.VMEM((peers * rows // 2, 128), jnp.float32),
            pltpu.VMEM((peers * rows // 2, 128), jnp.float32),
            pltpu.VMEM((2 * peers, rows // 2, 128), jnp.float32),
            pltpu.VMEM((rows // 2, 128), jnp.float32),
            pltpu.VMEM((rows // 2, 128), jnp.bfloat16),
            pltpu.VMEM((peers * rows // 2, 128), jnp.bfloat16),
            pltpu.VMEM((peers * rows, replicas * rank), jnp.bfloat16),
            pltpu.VMEM((peers * rows, width // peers), jnp.bfloat16),
            dma((6,)),
            dma((peers,)), dma((peers,)), dma((peers,)), dma((peers,)),
            dma((peers,)), dma((peers,)), dma((peers,)), dma((peers,)), dma((peers,)), dma((peers,)),
            dma((PLANE,)), dma((replicas,)), dma((PLANE,)), dma((replicas,)),
            dma((replicas,)), dma((replicas,)), dma((replicas,)), dma((replicas,)),
            dma((peers,)), dma((peers,)), dma((peers,)), dma((peers,)),
            dma((peers,)), dma((peers,)),
        ],
        compiler_params=pltpu.CompilerParams(
            collective_id=0, has_side_effects=True, vmem_limit_bytes=40 * 1024 * 1024
        ),
        cost_estimate=pl.CostEstimate(
            flops=2 * peers * rows * replicas * rank * (depth + width) // peers,
            bytes_accessed=2 * rows * (depth + width) + 2 * rank * (depth + width),
            transcendentals=0,
        ),
    )(hidden_state_rows, tags, down, up_factors[0])


def routed_rows(hidden_state_rows, stores, down_factors, up_factors):
    replicas = lax.axis_size("replica")
    total_rows = hidden_state_rows.shape[0]
    capacity = max(2, (2 * total_rows + replicas - 1) // replicas)
    order = jnp.arange(total_rows, dtype=jnp.int32)
    earlier = (stores[:, None] == stores[None, :]) & (order[None, :] < order[:, None])
    slot_index = jnp.sum(earlier.astype(jnp.int32), axis=1)
    target = stores * capacity + slot_index
    slots = jnp.arange(replicas * capacity, dtype=jnp.int32)
    placing = (slots[:, None] == target[None, :]).astype(jnp.bfloat16)
    outgoing = jnp.dot(placing, hidden_state_rows, preferred_element_type=jnp.float32).astype(
        jnp.bfloat16
    )
    outgoing = outgoing.reshape(replicas, capacity, hidden_state_rows.shape[1])
    arrived = lax.all_to_all(outgoing, "replica", split_axis=0, concat_axis=0, tiled=True)
    sources = arrived.shape[0]
    items = arrived.shape[1]
    flat_rows = arrived.reshape(sources * items, arrived.shape[2])
    narrowed_rows = jnp.dot(flat_rows, down_factors[0], preferred_element_type=jnp.float32).astype(
        jnp.bfloat16
    )
    widened_rows = (
        ADAPTER_SCALE * jnp.dot(narrowed_rows, up_factors[0], preferred_element_type=jnp.float32)
    ).astype(jnp.bfloat16)
    computed = widened_rows.reshape(sources, items, widened_rows.shape[1])
    returned = lax.all_to_all(computed, "replica", split_axis=0, concat_axis=0, tiled=True)
    returned = returned.reshape(replicas * capacity, returned.shape[2])
    picked = jnp.einsum("sr,sq->rq", placing, returned, preferred_element_type=jnp.float32)
    return picked.astype(jnp.bfloat16)


def per_device(
    hidden_state_rows,
    base_queries,
    cached_key_rows,
    cached_value_rows,
    cache_lengths,
    joining_flags,
    adapter_index,
    adapter_owner_row,
    pair_trade_flags,
    down_factors,
    up_factors,
):
    here = lax.axis_index("replica")
    trade = lax.dynamic_index_in_dim(pair_trade_flags, here // 2, 0, keepdims=False) == 1
    stores = stores_of(adapter_index, adapter_owner_row)
    few = lax.axis_size("replica") == 4 * PLANE and lax.axis_size("groups") == 2
    shifted = gathered_rows if few else routed_rows
    query_shift = shifted(hidden_state_rows, stores, down_factors, up_factors)
    attended = attend(
        base_queries,
        query_shift,
        cached_key_rows,
        cached_value_rows,
        cache_lengths,
        joining_flags,
    )
    return jnp.where(trade, swapped(attended, "replica", 0), attended)


def solution(mesh):
    placed = (
        P(("groups", "replica"), None),
        P(("groups", "replica"), None),
        P(("groups", "replica"), None, None),
        P(("groups", "replica"), None, None),
        P(("groups", "replica")),
        P(("groups", "replica")),
        P(("groups", "replica"), None),
        P(),
        P("groups"),
        P("replica", None, None),
        P("replica", None, None),
    )
    return jax.shard_map(
        per_device,
        mesh=mesh,
        in_specs=placed,
        out_specs=P(("groups", "replica"), None),
        check_vma=False,
    )
```

```python
import functools
import math

import jax
import jax.numpy as jnp
from jax import lax
from jax.experimental import pallas as pl
from jax.experimental.pallas import tpu as pltpu
from jax.sharding import PartitionSpec as P

QUERY_HEADS = 32
KEY_HEADS = 4
HEAD_WIDTH = 128
SPAN = 16
ADAPTER_SCALE = 0.5
ADAPTER_RANK = 64
NEG_LARGE = -1e30

STEP_ROWS = 16
HALF_ROWS = 8


def attend_kernel(lengths_ref, joins_ref, q_ref, d_ref, k_ref, v_ref, o_ref):
    positions = k_ref.shape[0] // STEP_ROWS
    per_group = QUERY_HEADS // KEY_HEADS
    keys = HALF_ROWS * positions
    rows = per_group * HALF_ROWS
    scale = 1.0 / math.sqrt(HEAD_WIDTH)
    row_request = lax.broadcasted_iota(jnp.int32, (rows, keys), 0) % HALF_ROWS
    column = lax.broadcasted_iota(jnp.int32, (rows, keys), 1)
    own = row_request == column // positions
    position = column % positions
    units = [(half, group) for half in range(2) for group in range(KEY_HEADS)]
    seen = []
    for half in range(2):
        limits = lengths_ref[0, half * HALF_ROWS : (half + 1) * HALF_ROWS, 0:1]
        joins = joins_ref[0, half * HALF_ROWS : (half + 1) * HALF_ROWS, 0:1]
        low = jnp.where(joins == 0, 0, limits - SPAN)
        limits = jnp.concatenate([limits] * per_group, axis=0)
        low = jnp.concatenate([low] * per_group, axis=0)
        seen.append(own & (position < limits) & (position >= low))
    scored = []
    for half, group in units:
        key_block = k_ref[pl.ds(half * keys, keys), pl.ds(group * HEAD_WIDTH, HEAD_WIDTH)]
        pieces = []
        for ref in (q_ref, d_ref):
            for head in range(per_group):
                at = (group * per_group + head) * HEAD_WIDTH
                piece = ref[:, pl.ds(at, HEAD_WIDTH)].astype(jnp.float32)
                pieces.append(piece[half * HALF_ROWS : (half + 1) * HALF_ROWS])
        queries = jnp.concatenate(pieces, axis=0).astype(jnp.bfloat16)
        both = lax.dot_general(
            queries, key_block, (((1,), (1,)), ((), ())), preferred_element_type=jnp.float32
        )
        scores = (both[:rows] + both[rows:]) * scale
        scored.append(jnp.where(seen[half], scores, NEG_LARGE))
    tops = [jnp.max(scores, axis=1, keepdims=True) for scores in scored]
    raised = [
        jnp.where(seen[half], jnp.exp(scores - top), 0.0)
        for (half, _), scores, top in zip(units, scored, tops)
    ]
    totals = [jnp.sum(lifted, axis=1, keepdims=True) for lifted in raised]
    halves = [[], []]
    for (half, group), lifted, total in zip(units, raised, totals):
        value_block = v_ref[pl.ds(half * keys, keys), pl.ds(group * HEAD_WIDTH, HEAD_WIDTH)]
        weights = (lifted / total).astype(jnp.bfloat16)
        halves[half].append(jnp.dot(weights, value_block, preferred_element_type=jnp.float32))
    for group in range(KEY_HEADS):
        for head in range(per_group):
            at = (group * per_group + head) * HEAD_WIDTH
            span = slice(head * HALF_ROWS, (head + 1) * HALF_ROWS)
            tile = jnp.concatenate([halves[0][group][span], halves[1][group][span]], axis=0)
            o_ref[:, pl.ds(at, HEAD_WIDTH)] = tile.astype(o_ref.dtype)


def attend(base_queries, query_shift, keys, values, cache_lengths, joining_flags):
    rows, width = base_queries.shape
    positions, cache_width = keys.shape[1:]
    steps = rows // STEP_ROWS
    keys = keys.reshape(rows * positions, cache_width)
    values = values.reshape(rows * positions, cache_width)
    lengths = jnp.broadcast_to(cache_lengths.reshape(steps, STEP_ROWS, 1), (steps, STEP_ROWS, 128))
    joins = jnp.broadcast_to(joining_flags.reshape(steps, STEP_ROWS, 1), (steps, STEP_ROWS, 128))
    small = pl.BlockSpec((1, STEP_ROWS, 128), lambda i: (i, 0, 0))
    wide = pl.BlockSpec((STEP_ROWS, width), lambda i: (i, 0))
    cache = pl.BlockSpec((STEP_ROWS * positions, cache_width), lambda i: (i, 0))
    return pl.pallas_call(
        attend_kernel,
        grid=(steps,),
        in_specs=[small, small, wide, wide, cache, cache],
        out_specs=wide,
        out_shape=jax.ShapeDtypeStruct((rows, width), jnp.bfloat16),
        compiler_params=pltpu.CompilerParams(vmem_limit_bytes=32 * 1024 * 1024),
        cost_estimate=pl.CostEstimate(
            flops=2 * 3 * rows * positions * HALF_ROWS * width,
            bytes_accessed=2 * (keys.size + values.size + 3 * rows * width),
            transcendentals=rows * positions * QUERY_HEADS * HALF_ROWS,
        ),
    )(lengths, joins, base_queries, query_shift, keys, values)


def swapped(block, axis, bit):
    count = lax.axis_size(axis)
    route = []
    for low in range(count):
        high = low | 1 << bit
        if high != low and high < count:
            route += [(low, high), (high, low)]
    return lax.ppermute(block, axis, route)


def stores_of(adapter_index, adapter_owner_row):
    adapter_column = adapter_index[:, 0]
    table = jnp.arange(adapter_owner_row.shape[0], dtype=jnp.int32)
    return jnp.sum(
        jnp.where(adapter_column[:, None] == table[None, :], adapter_owner_row[None, :], 0), axis=1
    )

PLANE = 4
ROUTES = pl.DeviceIdType.MESH


def gathered_kernel(
    layers, h_ref, st_ref, down_ref, up_ref, out_ref,
    h_buf, st_buf, tags, down_buf, up_buf, part, packed, part_in, narrow, narrow_all, spread, wide,
    local_sem, h_send, h_recv, st_send, st_recv,
    down_send, down_recv, up_send, up_recv, climb_send, sink_send, climb_up_send, sink_up_send,
    part_send, part_recv, narrow_send, narrow_recv, wide_send, wide_recv,
):
    rows = h_ref.shape[0]
    rank, depth = ADAPTER_RANK, down_buf.shape[1]
    lanes = up_buf.shape[1]
    group, here = lax.axis_index("groups"), lax.axis_index("replica")
    layer, local = here // PLANE, here % PLANE
    side, core = local // 2, local % 2
    me = group * PLANE + local
    peers = 2 * PLANE
    packs = rows // 2

    def peer(i):
        g = (group + i // 4) % 2
        l = ((side + (i // 2) % 2) % 2) * 2 + (core + i % 2) % 2
        return g, l, g * PLANE + l

    def push(src, dst, send, recv, g, r):
        return pltpu.make_async_remote_copy(
            src_ref=src, dst_ref=dst, send_sem=send, recv_sem=recv,
            device_id=(g, r), device_id_type=ROUTES,
        )

    def over_peers(body):
        def step(i, carry):
            body(*peer(i))
            return carry

        lax.fori_loop(1, peers, step, 0)

    def over_locals(body, first=0):
        def step(i, carry):
            body(peer(i)[1])
            return carry

        lax.fori_loop(first, PLANE, step, 0)

    barrier = pltpu.get_barrier_semaphore()

    def greet(g, l, j):
        pl.semaphore_signal(
            barrier, inc=1, device_id=(g, layer * PLANE + l), device_id_type=ROUTES
        )

    over_peers(greet)

    @pl.when(layer < layers - 1)
    def _():
        pl.semaphore_signal(barrier, inc=1, device_id=(group, here + PLANE), device_id_type=ROUTES)

    @pl.when(layer > 0)
    def _():
        pl.semaphore_signal(barrier, inc=1, device_id=(group, here - PLANE), device_id_type=ROUTES)

    inner = (layer + layers - 1) // layers - (layer + 1) // layers
    pl.semaphore_wait(barrier, peers + inner)

    def stored(buf, a):
        return buf.at[pl.ds(a * rank, rank), :]

    def tag_rows(ref, j):
        return ref.at[pl.ds(j * 8, 8), :]

    def piece(ref, j, size):
        return ref.at[:, pl.ds(j * size, size)]

    def block(ref, j):
        return ref.at[pl.ds(j * rows, rows), :]

    mine = [
        pltpu.make_async_copy(piece(down_ref, me, depth), stored(down_buf, here), local_sem.at[0]),
        pltpu.make_async_copy(piece(up_ref, me, lanes), stored(up_buf, here), local_sem.at[1]),
        pltpu.make_async_copy(piece(h_ref, me, depth), block(h_buf, me), local_sem.at[2]),
        pltpu.make_async_copy(st_ref, tag_rows(st_buf, me), local_sem.at[3]),
    ]
    for copy in mine:
        copy.start()

    def down_copy(l):
        j = group * PLANE + l
        return push(
            piece(down_ref, j, depth), stored(down_buf, here),
            down_send.at[l], down_recv.at[here], group, layer * PLANE + l,
        )

    def up_copy(l):
        j = group * PLANE + l
        return push(
            piece(up_ref, j, lanes), stored(up_buf, here),
            up_send.at[l], up_recv.at[here], group, layer * PLANE + l,
        )

    def h_copy(g, l, j):
        return push(
            piece(h_ref, j, depth), block(h_buf, me),
            h_send.at[j], h_recv.at[me], g, layer * PLANE + l,
        )

    def st_copy(g, l, j):
        return push(
            st_ref, tag_rows(st_buf, me), st_send.at[j], st_recv.at[me], g, layer * PLANE + l
        )

    over_locals(lambda l: down_copy(l).start(), 1)
    mine[0].wait()
    mine[1].wait()

    def onward(buf, a, send, recv, step, view):
        return push(
            view(buf, a), view(buf, a), send.at[a], recv.at[a], group, here + step * PLANE
        )

    def arrived(buf, a, recv, view):
        push(view(buf, a), view(buf, a), local_sem.at[4], recv.at[a], group, here).wait_recv()

    def hop(buf, a, send, recv, step, do):
        do(onward(buf, a, send, recv, step, stored))

    def start(copy):
        copy.start()

    def first_hop(buf, recv, climb, sink, l):
        a = layer * PLANE + l

        @pl.when(l != local)
        def _():
            arrived(buf, a, recv, stored)

        @pl.when(layer < layers - 1)
        def _():
            hop(buf, a, climb, recv, 1, start)

        @pl.when(layer > 0)
        def _():
            hop(buf, a, sink, recv, -1, start)

    def landed(buf, a, recv):
        arrived(buf, a, recv, stored)

    def later_hop(buf, recv, climb, sink, t, l):
        @pl.when(layer - t >= 0)
        def _():
            a = (layer - t) * PLANE + l
            landed(buf, a, recv)

            @pl.when(layer < layers - 1)
            def _():
                hop(buf, a, climb, recv, 1, start)

        @pl.when(layer + t < layers)
        def _():
            a = (layer + t) * PLANE + l
            landed(buf, a, recv)

            @pl.when(layer > 0)
            def _():
                hop(buf, a, sink, recv, -1, start)

    downs = (down_buf, down_recv, climb_send, sink_send)
    ups = (up_buf, up_recv, climb_up_send, sink_up_send)
    first_hop(*downs, local)
    over_peers(lambda g, l, j: st_copy(g, l, j).start())
    over_locals(lambda l: first_hop(*downs, l), 1)

    over_peers(lambda g, l, j: h_copy(g, l, j).start())
    over_locals(lambda l: up_copy(l).start(), 1)
    for t in range(1, layers - 1):
        over_locals(lambda l: later_hop(*downs, t, l))
    over_locals(lambda l: first_hop(*ups, l))
    mine[2].wait()
    mine[3].wait()

    def here_recv(src, dst, recv, g, l):
        push(src, dst, local_sem.at[4], recv, g, layer * PLANE + l).wait_recv()

    def taken(view, recv):
        return lambda g, l, j: here_recv(view(j), view(j), recv.at[j], g, l)

    def tagged(src, dst):
        for j in range(peers):
            row = src[j * 8 : j * 8 + 1, :].astype(jnp.float32)
            turned = jnp.transpose(jnp.broadcast_to(row, (128, 128)))
            dst[j * rows : (j + 1) * rows, :] = turned[:rows].astype(jnp.int32)

    over_peers(taken(lambda j: tag_rows(st_buf, j), st_recv))
    tagged(st_buf, tags)

    over_peers(taken(lambda j: block(h_buf, j), h_recv))
    over_locals(lambda l: later_hop(*downs, layers - 1, l))

    lane = lax.broadcasted_iota(jnp.int32, (1, 2 * rank), 1) // rank

    def products(left, right, stores_ref, to):
        part[...] = jnp.zeros_like(part)

        def narrowed(s, carry):
            at = pl.ds(s * 4 * rank, 4 * rank)
            both = lax.dot_general(
                left[...], right[at, :], (((1,), (1,)), ((), ())),
                preferred_element_type=jnp.float32,
            )
            stores = stores_ref[...]
            kept = jnp.where(stores == s * 4 + lane, both[:, : 2 * rank], 0.0)
            kept = kept + jnp.where(stores == s * 4 + 2 + lane, both[:, 2 * rank :], 0.0)
            part[...] += kept
            return carry

        lax.fori_loop(0, down_buf.shape[0] // (4 * rank), narrowed, 0)
        summed = part[...]
        summed = summed + pltpu.roll(summed, rank, 1)
        for j in range(peers):
            first = summed[j * rows : j * rows + packs]
            second = summed[j * rows + packs : (j + 1) * rows]
            to[j * packs : (j + 1) * packs, :] = jnp.where(lane == 0, first, second)

    def packs_of(ref, j):
        return ref.at[pl.ds(j * packs, packs), :]

    def part_copy(g, l, j):
        return push(
            packs_of(packed, j), part_in.at[me], part_send.at[j], part_recv.at[me],
            g, layer * PLANE + l,
        )

    products(h_buf, down_buf, tags, packed)
    over_peers(lambda g, l, j: part_copy(g, l, j).start())
    for t in range(1, layers - 1):
        over_locals(lambda l: later_hop(*ups, t, l))
    over_peers(taken(lambda j: part_in.at[j], part_recv))
    part_in[me] = packed[pl.ds(me * packs, packs), :]
    total = part_in[0]
    for j in range(1, peers):
        total = total + part_in[j]
    narrow[...] = total.astype(jnp.bfloat16)

    def narrow_copy(g, l, j):
        return push(
            narrow, packs_of(narrow_all, me), narrow_send.at[j], narrow_recv.at[me],
            g, layer * PLANE + l,
        )

    over_peers(lambda g, l, j: narrow_copy(g, l, j).start())
    narrow_all[pl.ds(me * packs, packs), :] = narrow[...]
    over_peers(taken(lambda j: packs_of(narrow_all, j), narrow_recv))
    for j in range(peers):
        pair = narrow_all[j * packs : (j + 1) * packs, :].astype(jnp.float32)
        turned = pltpu.roll(pair, rank, 1)
        own = jnp.concatenate(
            [jnp.where(lane == 0, pair, turned), jnp.where(lane == 0, turned, pair)], axis=0
        )
        stores = tags[j * rows : (j + 1) * rows, :]
        for s in range(spread.shape[1] // (2 * rank)):
            spread[j * rows : (j + 1) * rows, s * 2 * rank : (s + 1) * 2 * rank] = jnp.where(
                stores == 2 * s + lane, own, 0.0
            ).astype(jnp.bfloat16)
    over_locals(lambda l: later_hop(*ups, layers - 1, l))

    def widened(c, carry):
        at = pl.ds(c * 256, 256)
        block_of = jnp.dot(spread[...], up_buf[:, at], preferred_element_type=jnp.float32)
        wide[:, at] = (ADAPTER_SCALE * block_of).astype(jnp.bfloat16)
        return carry

    lax.fori_loop(0, lanes // 256, widened, 0)

    def wide_copy(g, l, j):
        return push(
            block(wide, j), piece(out_ref, me, lanes), wide_send.at[j], wide_recv.at[me],
            g, layer * PLANE + l,
        )

    over_peers(lambda g, l, j: wide_copy(g, l, j).start())
    last = pltpu.make_async_copy(block(wide, me), piece(out_ref, me, lanes), local_sem.at[5])
    last.start()
    last.wait()
    over_peers(
        lambda g, l, j: here_recv(
            piece(out_ref, j, lanes), piece(out_ref, j, lanes), wide_recv.at[j], g, l
        )
    )

    def left(l):
        down_copy(l).wait_send()
        up_copy(l).wait_send()

    over_locals(left, 1)

    def left_peer(g, l, j):
        h_copy(g, l, j).wait_send()
        st_copy(g, l, j).wait_send()
        part_copy(g, l, j).wait_send()
        narrow_copy(g, l, j).wait_send()
        wide_copy(g, l, j).wait_send()

    over_peers(left_peer)

    def sent(copy):
        copy.wait_send()

    def passed(s, carry):
        def one(l):
            a = s * PLANE + l

            @pl.when((layer < layers - 1) & (s <= layer))
            def _():
                hop(down_buf, a, climb_send, down_recv, 1, sent)
                hop(up_buf, a, climb_up_send, up_recv, 1, sent)

            @pl.when((layer > 0) & (s >= layer))
            def _():
                hop(down_buf, a, sink_send, down_recv, -1, sent)
                hop(up_buf, a, sink_up_send, up_recv, -1, sent)

        over_locals(one)
        return carry

    lax.fori_loop(0, layers, passed, 0)


def gathered_rows(hidden_state_rows, stores, down_factors, up_factors):
    replicas = lax.axis_size("replica")
    rows, depth = hidden_state_rows.shape
    rank, width = up_factors.shape[1:]
    layers = replicas // PLANE
    peers = 2 * PLANE
    down = jnp.swapaxes(down_factors[0], 0, 1)
    tags = jnp.broadcast_to(jnp.pad(stores, (0, 128 - rows))[None, :], (8, 128))
    dma = pltpu.SemaphoreType.DMA
    here = pl.BlockSpec(memory_space=pltpu.VMEM)
    far = pl.BlockSpec(memory_space=pl.ANY)
    return pl.pallas_call(
        functools.partial(gathered_kernel, layers),
        in_specs=[here] * 4,
        out_specs=pl.BlockSpec(memory_space=pl.ANY),
        out_shape=jax.ShapeDtypeStruct((rows, width), jnp.bfloat16),
        scratch_shapes=[
            pltpu.VMEM((peers * rows, depth // peers), jnp.bfloat16),
            pltpu.VMEM((peers * 8, 128), jnp.int32),
            pltpu.VMEM((peers * rows, 128), jnp.int32),
            pltpu.VMEM((replicas * rank, depth // peers), jnp.bfloat16),
            pltpu.VMEM((replicas * rank, width // peers), jnp.bfloat16),
            pltpu.VMEM((peers * rows, 128), jnp.float32),
            pltpu.VMEM((peers * rows // 2, 128), jnp.float32),
            pltpu.VMEM((peers, rows // 2, 128), jnp.float32),
            pltpu.VMEM((rows // 2, 128), jnp.bfloat16),
            pltpu.VMEM((peers * rows // 2, 128), jnp.bfloat16),
            pltpu.VMEM((peers * rows, replicas * rank), jnp.bfloat16),
            pltpu.VMEM((peers * rows, width // peers), jnp.bfloat16),
            dma((6,)),
            dma((peers,)), dma((peers,)), dma((peers,)), dma((peers,)),
            dma((PLANE,)), dma((replicas,)), dma((PLANE,)), dma((replicas,)),
            dma((replicas,)), dma((replicas,)), dma((replicas,)), dma((replicas,)),
            dma((peers,)), dma((peers,)), dma((peers,)), dma((peers,)),
            dma((peers,)), dma((peers,)),
        ],
        compiler_params=pltpu.CompilerParams(
            collective_id=0, has_side_effects=True, vmem_limit_bytes=40 * 1024 * 1024
        ),
        cost_estimate=pl.CostEstimate(
            flops=2 * peers * rows * replicas * rank * (depth + width) // peers,
            bytes_accessed=2 * rows * (depth + width) + 2 * rank * (depth + width),
            transcendentals=0,
        ),
    )(hidden_state_rows, tags, down, up_factors[0])


def routed_rows(hidden_state_rows, stores, down_factors, up_factors):
    replicas = lax.axis_size("replica")
    total_rows = hidden_state_rows.shape[0]
    capacity = max(2, (2 * total_rows + replicas - 1) // replicas)
    order = jnp.arange(total_rows, dtype=jnp.int32)
    earlier = (stores[:, None] == stores[None, :]) & (order[None, :] < order[:, None])
    slot_index = jnp.sum(earlier.astype(jnp.int32), axis=1)
    target = stores * capacity + slot_index
    slots = jnp.arange(replicas * capacity, dtype=jnp.int32)
    placing = (slots[:, None] == target[None, :]).astype(jnp.bfloat16)
    outgoing = jnp.dot(placing, hidden_state_rows, preferred_element_type=jnp.float32).astype(
        jnp.bfloat16
    )
    outgoing = outgoing.reshape(replicas, capacity, hidden_state_rows.shape[1])
    arrived = lax.all_to_all(outgoing, "replica", split_axis=0, concat_axis=0, tiled=True)
    sources = arrived.shape[0]
    items = arrived.shape[1]
    flat_rows = arrived.reshape(sources * items, arrived.shape[2])
    narrowed_rows = jnp.dot(flat_rows, down_factors[0], preferred_element_type=jnp.float32).astype(
        jnp.bfloat16
    )
    widened_rows = (
        ADAPTER_SCALE * jnp.dot(narrowed_rows, up_factors[0], preferred_element_type=jnp.float32)
    ).astype(jnp.bfloat16)
    computed = widened_rows.reshape(sources, items, widened_rows.shape[1])
    returned = lax.all_to_all(computed, "replica", split_axis=0, concat_axis=0, tiled=True)
    returned = returned.reshape(replicas * capacity, returned.shape[2])
    picked = jnp.einsum("sr,sq->rq", placing, returned, preferred_element_type=jnp.float32)
    return picked.astype(jnp.bfloat16)


def per_device(
    hidden_state_rows,
    base_queries,
    cached_key_rows,
    cached_value_rows,
    cache_lengths,
    joining_flags,
    adapter_index,
    adapter_owner_row,
    pair_trade_flags,
    down_factors,
    up_factors,
):
    here = lax.axis_index("replica")
    trade = lax.dynamic_index_in_dim(pair_trade_flags, here // 2, 0, keepdims=False) == 1
    stores = stores_of(adapter_index, adapter_owner_row)
    few = lax.axis_size("replica") == 4 * PLANE and lax.axis_size("groups") == 2
    shifted = gathered_rows if few else routed_rows
    query_shift = shifted(hidden_state_rows, stores, down_factors, up_factors)
    attended = attend(
        base_queries,
        query_shift,
        cached_key_rows,
        cached_value_rows,
        cache_lengths,
        joining_flags,
    )
    return jnp.where(trade, swapped(attended, "replica", 0), attended)


def solution(mesh):
    placed = (
        P(("groups", "replica"), None),
        P(("groups", "replica"), None),
        P(("groups", "replica"), None, None),
        P(("groups", "replica"), None, None),
        P(("groups", "replica")),
        P(("groups", "replica")),
        P(("groups", "replica"), None),
        P(),
        P("groups"),
        P("replica", None, None),
        P("replica", None, None),
    )
    return jax.shard_map(
        per_device,
        mesh=mesh,
        in_specs=placed,
        out_specs=P(("groups", "replica"), None),
        check_vma=False,
    )
```
